32 devices in a mesh: segment: 2 (over core), expert: 16 (over z, y, x).
Axes of the slice: x: 2, y: 2, z: 4, core: 2. Of those that a mesh axis runs over, the one named last changes fastest.
Arguments:
- tokens: bfloat16 [2, 1024, 2048], P(None, 'expert'), may hold values from -6 to 6
- routing: int32 [2, 2, 1024, 8], P(None, None, 'expert'), may hold values from 0 to 15, all different within a row; in each aligned block of 64 rows (0 to 63, 64 to 127, ..., all dimensions but the last counted through in order) at most 64 rows name the same one
- norm_gain: bfloat16 [2, 2048], P('segment'), may hold values from 0.5 to 1.5
- router_weight: bfloat16 [2, 2048, 16], P('segment'), may hold values from -0.125 to 0.125
- expert_gate_up: bfloat16 [2, 16, 2048, 768], P('segment', 'expert'), may hold values from -0.125 to 0.125
- expert_down: bfloat16 [2, 16, 384, 2048], P('segment', 'expert'), may hold values from -0.3125 to 0.3125
- pair_index: int32 [64], replicated, may hold values from 0 to 63, each once
- topic_ids: int32 [64], replicated, may hold values from 0 to 7
Outputs:
- final_hidden: bfloat16 [2, 1024, 2048], P('segment', 'expert')
- query_loss: float32 [64], P(('segment', 'expert'))
The draws below stay inside these ranges and needn't reach their ends.
Inputs may be any that keep to these rules, and one draw needn't show every extreme that they name: `routing`: each row names 8 different experts. In the rows of one device (each aligned block of 64 token rows of one layer and micro-batch) no expert is named by more than 64 rows, a bound that some block reaches. `pair_index`: every passage is the positive of exactly one query.
All inputs are finite; a program needn't handle non-finite values.
Results may differ from the reference program's by a relative error of at most 0.0059.
Values may be sent and summed in bfloat16 or wider, within the bound.
A program may use at most 128 MiB of HBM per device.

```python
import math
import jax
import jax.numpy as jnp
import numpy as np
from jax import lax

D = 2048
FF = 384
TOPK = 8
SEQ = 16
TOPICS = 8
TOK_DEV = 64
EXPERTS = 16
MICRO = 2
TOKENS = 1024
CAP = 64
HALF = 2
PAIRS = 64
N_SEGMENT = 2
N_EXPERT = 16


def draw_tokens(key, part):
    direction_key = jax.random.fold_in(key, 11)
    choice_key = jax.random.fold_in(key, 23)
    noise_key = jax.random.fold_in(key, 37)
    sequence_count = TOKENS // SEQ
    directions = jax.random.normal(direction_key, (64, D), jnp.float32)
    picked_ids = jax.random.randint(choice_key, (MICRO, sequence_count), 0, 64)
    offsets = directions[picked_ids]
    noise = jax.random.normal(noise_key, (MICRO, sequence_count, SEQ, D), jnp.float32)
    strength = 0.3
    rows = noise + strength * offsets[:, :, None, :]
    rows = jnp.clip(rows, -6.0, 6.0)
    return rows.reshape(MICRO, TOKENS, D).astype(jnp.bfloat16)


def place_ends(result, stream_key, least, largest):
    index_at = [jax.random.randint(jax.random.fold_in(stream_key, axis), (), 0, length) for axis, length in enumerate(result.shape)]
    main_axis = result.shape.index(max(result.shape))
    beside = index_at[:main_axis] + [(index_at[main_axis] + 1) % result.shape[main_axis]] + index_at[main_axis + 1:]
    return result.at[tuple(index_at)].set(least).at[tuple(beside)].set(largest)


def steps_of(own_key, dims, split, low, high):
    gain = 1.0
    for axis_at, blocks in split:
        heights = jax.random.uniform(jax.random.fold_in(jax.random.fold_in(own_key, 6), axis_at), (blocks,), jnp.float32, low / len(split), high / len(split))
        gain = gain * jnp.repeat(jnp.exp(heights), dims[axis_at] // blocks).reshape((-1,) + (1,) * (len(dims) - 1 - axis_at))
    return gain


def deal_out(own_key, own, number, rows, amount, top, limit, skew):
    order = jax.random.permutation(own_key, amount)
    packed, ordinary = shares(amount, rows * top, limit, skew, True), shares(amount, rows * top, limit, skew, False)
    places = jnp.arange(amount)

    def named(lengths, rotation):
        used = int((lengths > 0).sum())
        fixed = max(1, used // 4)
        moved = fixed + (places - fixed + rotation * (used - fixed)) % max(1, amount - fixed)
        return jnp.zeros((amount,), jnp.int32).at[order[jnp.where(places < fixed, places, moved)]].set(jnp.asarray(lengths, jnp.int32))

    lengths = jnp.where(number % 4 == 0, named(packed, number // 4), named(ordinary, number - number // 4 - 1))
    mixed = jax.random.permutation(jax.random.fold_in(own, 3), amount)
    source_of, receiver = mixed[0:amount // 2 * 2:2], mixed[1:amount // 2 * 2:2]
    margin = jnp.minimum(lengths[source_of] - 1, limit - lengths[receiver]) // 2
    margin = jnp.where((source_of == order[0]) | (receiver == order[0]) | (lengths[receiver] == 0), 0, jnp.maximum(margin, 0))
    moved = jax.random.randint(jax.random.fold_in(own, 4), (amount // 2,), 0, 1 << 20) % (margin + 1)
    lengths = lengths.at[source_of].add(-moved).at[receiver].add(moved)
    labels = jnp.searchsorted(jnp.cumsum(lengths), jnp.arange(rows * top), side="right").astype(jnp.int32)
    table = labels.reshape(top, rows).T
    table = table[jax.random.permutation(jax.random.fold_in(own, 1), rows)]
    rotation = jax.random.randint(jax.random.fold_in(own, 2), (rows, 1), 0, top)
    return jnp.take_along_axis(table, (jnp.arange(top)[None, :] + rotation) % top, axis=1)


def shares(number_of, total, reach, slope, full):
    weights = [(1 << 20) // math.isqrt(rank ** slope) + 1 for rank in range(1, number_of + 1)]
    largest = reach if full else min(reach, max(-(-total // number_of), total * weights[0] // sum(weights)))
    least = 1 if total - largest >= number_of - 1 else 0
    counts, spare = [largest] + [least] * (number_of - 1), total - largest - least * (number_of - 1)
    while spare > 0:
        free = [i for i in range(1, number_of) if counts[i] < largest] or [i for i in range(1, number_of) if counts[i] < reach]
        mass, remaining = sum([weights[i] for i in free]), spare
        for i in free:
            extra = min(reach - counts[i], max(1, remaining * weights[i] // mass), spare)
            counts[i] = counts[i] + extra
            spare = spare - extra
    return np.array(counts)


def normal_values(key, extent, scale, bound, split=(), kind=jnp.bfloat16):
    loudness = steps_of(key, extent, split, -0.22, 0.18) if split else 1.0
    result = jax.random.normal(key, extent, jnp.float32) * scale * loudness
    return jnp.minimum(jnp.maximum(result, -bound), bound).astype(kind)


def setup_inputs(seed: int = 0) -> dict:
    seeds = jax.random.split(jax.random.key(seed), 9)
    tokens = draw_tokens(jax.random.fold_in(seeds[8], 71), 0)
    routing_keys = jax.random.split(jax.random.fold_in(seeds[1], 1), N_SEGMENT * MICRO * TOKENS // TOK_DEV)
    routing_turns = jax.random.permutation(jax.random.fold_in(seeds[1], 3), N_SEGMENT * MICRO * TOKENS // TOK_DEV)
    routing = jax.vmap(lambda own, number: deal_out(jax.random.fold_in(seeds[1], 2), own, number, TOK_DEV, EXPERTS, TOPK, CAP, 2))(routing_keys, routing_turns).reshape((N_SEGMENT, MICRO, TOKENS, TOPK))
    norm_gain = jnp.clip(1.0 + 0.1 * jax.random.normal(seeds[2], (N_SEGMENT, D), jnp.float32), 0.5, 1.5).astype(jnp.bfloat16)
    router_weight = normal_values(seeds[3], (N_SEGMENT, D, EXPERTS), D ** -0.5, 0.125, ((0, 2),))
    expert_gate_up = normal_values(seeds[4], (N_SEGMENT, EXPERTS, D, 2 * FF), D ** -0.5, 0.125, ((0, 2), (1, 16)))
    expert_down = normal_values(seeds[5], (N_SEGMENT, EXPERTS, FF, D), FF ** -0.5, 0.3125, ((0, 2), (1, 16)))
    pair_index = jax.random.permutation(seeds[6], PAIRS).astype(jnp.int32)
    topic_ids = place_ends(jax.random.randint(seeds[7], (PAIRS,), 0, TOPICS), jax.random.fold_in(seeds[7], 1), 0, TOPICS - 1).astype(jnp.int32)
    return {"tokens": tokens, "routing": routing, "norm_gain": norm_gain, "router_weight": router_weight, "expert_gate_up": expert_gate_up, "expert_down": expert_down, "pair_index": pair_index, "topic_ids": topic_ids}


EPSILON = 1e-06
SOFTMAX_WARMTH = 0.05

def reference_layer(inputs, routes, norm_gain, router_weight, gate_up, down_proj):
    widened = inputs.astype(jnp.float32)
    normed = (widened * lax.rsqrt(lax.optimization_barrier(jnp.mean(widened * widened, axis=1, keepdims=True)) + EPSILON) * norm_gain.astype(jnp.float32)).astype(jnp.bfloat16)
    similarity_logits = jnp.dot(normed, router_weight, preferred_element_type=jnp.float32)
    chosen = jnp.take_along_axis(similarity_logits, routes, axis=1)
    raised = jnp.exp(chosen)
    gate_weights = raised / lax.optimization_barrier(jnp.sum(raised, axis=1, keepdims=True))
    block_ids = routes.reshape(N_EXPERT, TOK_DEV * TOPK)
    one_hot = (block_ids[:, :, None] == jnp.arange(EXPERTS, dtype=jnp.int32)[None, None, :]).astype(jnp.int32)
    earlier = jnp.cumsum(one_hot, axis=1) - one_hot
    slot_index = lax.optimization_barrier(jnp.sum(earlier * one_hot, axis=2))
    source = jnp.arange(N_EXPERT, dtype=jnp.int32)[:, None]
    position = (block_ids * (N_EXPERT * CAP) + source * CAP + slot_index).reshape(-1)
    token_number = jnp.repeat(jnp.arange(TOKENS, dtype=jnp.int32), TOPK)
    slot_table = jnp.zeros((EXPERTS * N_EXPERT * CAP,), jnp.int32).at[position].set(token_number + 1)
    slot_table = slot_table.reshape(EXPERTS, N_EXPERT * CAP)

    def one_expert(operands):
        entries, expert_gate, expert_proj = operands
        gathered = normed[jnp.maximum(entries - 1, 0)]
        gathered = jnp.where((entries > 0)[:, None], gathered, jnp.zeros_like(gathered))
        projected = jnp.dot(gathered, expert_gate, preferred_element_type=jnp.float32)
        hidden = (jax.nn.silu(projected[:, :FF]) * projected[:, FF:]).astype(jnp.bfloat16)
        return jnp.dot(hidden, expert_proj, preferred_element_type=jnp.float32).astype(jnp.bfloat16)
    answers = lax.map(one_expert, (slot_table, gate_up, down_proj)).reshape(-1, D)
    position = position.reshape(TOKENS, TOPK)
    mixture = jnp.zeros((TOKENS, D), jnp.float32)
    for top_index in range(TOPK):
        picked = answers[position[:, top_index]].astype(jnp.float32)
        mixture = mixture + gate_weights[:, top_index][:, None] * picked
    return (widened + mixture).astype(jnp.bfloat16)

def reference(tokens, routing, norm_gain, router_weight, expert_gate_up, expert_down, pair_index, topic_ids):
    states = [tokens[micro_index] for micro_index in range(MICRO)]
    for layer_index in range(N_SEGMENT):
        states = [reference_layer(states[micro_index], routing[layer_index, micro_index], norm_gain[layer_index], router_weight[layer_index], expert_gate_up[layer_index], expert_down[layer_index]) for micro_index in range(MICRO)]
    final_hidden = jnp.stack(states)
    widened = final_hidden.astype(jnp.float32).reshape(MICRO, TOKENS // SEQ, SEQ, D)
    pooled = lax.optimization_barrier(jnp.mean(widened, axis=2))
    embedded = (pooled * lax.rsqrt(lax.optimization_barrier(jnp.sum(pooled * pooled, axis=2, keepdims=True)) + EPSILON)).astype(jnp.bfloat16)
    grouped = embedded.reshape(MICRO, N_EXPERT, 2, HALF, D)
    query_vectors = grouped[:, :, 0].reshape(PAIRS, D)
    passage_vectors = grouped[:, :, 1].reshape(PAIRS, D)
    pair_scores = jnp.dot(query_vectors, passage_vectors.T, preferred_element_type=jnp.float32) / SOFTMAX_WARMTH
    columns = jnp.arange(PAIRS, dtype=jnp.int32)
    is_positive = pair_index[:, None] == columns[None, :]
    positive_topic = topic_ids[pair_index]
    kept_pairs = is_positive | (topic_ids[None, :] != positive_topic[:, None])
    partition = lax.optimization_barrier(jnp.sum(jnp.where(kept_pairs, jnp.exp(pair_scores), jnp.zeros_like(pair_scores)), axis=1))
    positive = lax.optimization_barrier(jnp.sum(jnp.where(is_positive, pair_scores, jnp.zeros_like(pair_scores)), axis=1))
    return (final_hidden, jnp.log(partition) - positive)
```

```python
import jax
import jax.numpy as jnp
from jax import lax
from jax.sharding import PartitionSpec as P

SEQ = 16


EPSILON = 1e-06
SOFTMAX_WARMTH = 0.05


def pooled_embeddings(final_rows):
    widened = final_rows.astype(jnp.float32)
    pooled = jnp.mean(widened.reshape(-1, SEQ, widened.shape[1]), axis=1)
    return (pooled * lax.rsqrt(jnp.sum(pooled * pooled, axis=1, keepdims=True) + EPSILON)).astype(
        jnp.bfloat16
    )


def normalised(rows, gain):
    widened = rows.astype(jnp.float32)
    return (
        widened
        * lax.rsqrt(jnp.mean(widened * widened, axis=1, keepdims=True) + EPSILON)
        * gain.astype(jnp.float32)
    ).astype(jnp.bfloat16)


def dense_gates(normed, routes, router_weight):
    expert_count = router_weight.shape[1]
    logits = jnp.dot(normed, router_weight, preferred_element_type=jnp.float32)
    experts = jnp.arange(expert_count, dtype=jnp.int32)
    named = jnp.any(routes[:, :, None] == experts[None, None, :], axis=1)
    raised = jnp.where(named, jnp.exp(logits), 0.0)
    return raised / jnp.sum(raised, axis=1, keepdims=True)


def contrastive(final_rows, pair_index, topic_ids):
    embedded = pooled_embeddings(final_rows)
    half_count = embedded.shape[0] // 2
    own_queries = embedded[:half_count]
    passages = lax.all_gather(embedded[half_count:], ("segment", "expert"), axis=0, tiled=True)
    device_flat = lax.axis_index(("segment", "expert"))
    positive = lax.dynamic_slice_in_dim(pair_index, device_flat * half_count, half_count)
    columns = jnp.arange(topic_ids.shape[0], dtype=jnp.int32)
    is_positive = positive[:, None] == columns[None, :]
    positive_topic = jnp.sum(jnp.where(is_positive, topic_ids[None, :], 0), axis=1)
    kept = is_positive | (topic_ids[None, :] != positive_topic[:, None])
    scores = (
        jnp.dot(own_queries, passages.T, preferred_element_type=jnp.float32) / SOFTMAX_WARMTH
    )
    partition = jnp.sum(jnp.where(kept, jnp.exp(scores), 0.0), axis=1)
    return jnp.log(partition) - jnp.sum(jnp.where(is_positive, scores, 0.0), axis=1)


def gathered(
    tokens, routing, norm_gain, router_weight, expert_gate_up, expert_down, pair_index, topic_ids
):
    segment_index = lax.axis_index("segment")
    expert_index = lax.axis_index("expert")
    gains = lax.all_gather(norm_gain, "segment", axis=0, tiled=True)
    routers = lax.all_gather(router_weight, "segment", axis=0, tiled=True)

    def by_layer(own):
        other = lax.ppermute(own, "segment", [(0, 1), (1, 0)])
        first = segment_index == 0
        return jnp.where(first, own, other), jnp.where(first, other, own)

    gate_ups = by_layer(expert_gate_up[0, 0])
    downs = by_layer(expert_down[0, 0])
    rows = lax.dynamic_index_in_dim(tokens, segment_index, 0, keepdims=False)
    micro_routes = lax.dynamic_index_in_dim(routing, segment_index, 1, keepdims=False)
    half_width = expert_down.shape[2]
    for layer in range(routing.shape[0]):
        normed = normalised(rows, gains[layer])
        gates = dense_gates(normed, micro_routes[layer], routers[layer])
        own_gate = lax.all_to_all(gates, "expert", split_axis=1, concat_axis=0, tiled=True)
        everyone = lax.all_gather(normed, "expert", axis=0, tiled=True)
        projected = jnp.dot(everyone, gate_ups[layer], preferred_element_type=jnp.float32)
        hidden = (
            jax.nn.silu(projected[:, :half_width]) * projected[:, half_width:]
        ).astype(jnp.bfloat16)
        answer = jnp.dot(hidden, downs[layer], preferred_element_type=jnp.float32)
        part = (answer * own_gate).astype(jnp.bfloat16)
        mixture = lax.psum_scatter(part, "expert", scatter_dimension=0, tiled=True)
        rows = (rows.astype(jnp.float32) + mixture.astype(jnp.float32)).astype(jnp.bfloat16)
    return rows[None], contrastive(rows, pair_index, topic_ids)


def solution(mesh):
    in_specs = (
        P(None, "expert", None),
        P(None, None, "expert", None),
        P("segment", None),
        P("segment", None, None),
        P("segment", "expert", None, None),
        P("segment", "expert", None, None),
        P(),
        P(),
    )
    out_specs = (P("segment", "expert", None), P(("segment", "expert")))
    return jax.shard_map(gathered, mesh=mesh, in_specs=in_specs, out_specs=out_specs, check_vma=False)
```

```python
import functools

import jax
import jax.numpy as jnp
from jax import lax
from jax.experimental import pallas as pl
from jax.experimental.pallas import tpu as pltpu
from jax.sharding import PartitionSpec as P

SEQ = 16


EPSILON = 1e-06
SOFTMAX_WARMTH = 0.05


def pooled_embeddings(final_rows):
    widened = final_rows.astype(jnp.float32)
    pooled = jnp.mean(widened.reshape(-1, SEQ, widened.shape[1]), axis=1)
    return (pooled * lax.rsqrt(jnp.sum(pooled * pooled, axis=1, keepdims=True) + EPSILON)).astype(
        jnp.bfloat16
    )


def normalised(rows, gain):
    widened = rows.astype(jnp.float32)
    return (
        widened
        * lax.rsqrt(jnp.mean(widened * widened, axis=1, keepdims=True) + EPSILON)
        * gain.astype(jnp.float32)
    ).astype(jnp.bfloat16)


def dense_gates(normed, routes, router_weight):
    expert_count = router_weight.shape[1]
    logits = jnp.dot(normed, router_weight, preferred_element_type=jnp.float32)
    experts = jnp.arange(expert_count, dtype=jnp.int32)
    named = jnp.any(routes[:, :, None] == experts[None, None, :], axis=1)
    raised = jnp.where(named, jnp.exp(logits), 0.0)
    return raised / jnp.sum(raised, axis=1, keepdims=True)


def contrastive(final_rows, pair_index, topic_ids, passages=None):
    embedded = pooled_embeddings(final_rows)
    half_count = embedded.shape[0] // 2
    own_queries = embedded[:half_count]
    if passages is None:
        passages = lax.all_gather(embedded[half_count:], ("segment", "expert"), axis=0, tiled=True)
    device_flat = lax.axis_index(("segment", "expert"))
    positive = lax.dynamic_slice_in_dim(pair_index, device_flat * half_count, half_count)
    columns = jnp.arange(topic_ids.shape[0], dtype=jnp.int32)
    is_positive = positive[:, None] == columns[None, :]
    positive_topic = jnp.sum(jnp.where(is_positive, topic_ids[None, :], 0), axis=1)
    kept = is_positive | (topic_ids[None, :] != positive_topic[:, None])
    scores = (
        jnp.dot(own_queries, passages.T, preferred_element_type=jnp.float32) / SOFTMAX_WARMTH
    )
    partition = jnp.sum(jnp.where(kept, jnp.exp(scores), 0.0), axis=1)
    return jnp.log(partition) - jnp.sum(jnp.where(is_positive, scores, 0.0), axis=1)


def gathered(
    tokens, routing, norm_gain, router_weight, expert_gate_up, expert_down, pair_index, topic_ids
):
    segment_index = lax.axis_index("segment")
    expert_index = lax.axis_index("expert")
    gains = lax.all_gather(norm_gain, "segment", axis=0, tiled=True)
    routers = lax.all_gather(router_weight, "segment", axis=0, tiled=True)

    def by_layer(own):
        other = lax.ppermute(own, "segment", [(0, 1), (1, 0)])
        first = segment_index == 0
        return jnp.where(first, own, other), jnp.where(first, other, own)

    gate_ups = by_layer(expert_gate_up[0, 0])
    downs = by_layer(expert_down[0, 0])
    rows = lax.dynamic_index_in_dim(tokens, segment_index, 0, keepdims=False)
    micro_routes = lax.dynamic_index_in_dim(routing, segment_index, 1, keepdims=False)
    half_width = expert_down.shape[2]
    for layer in range(routing.shape[0]):
        normed = normalised(rows, gains[layer])
        gates = dense_gates(normed, micro_routes[layer], routers[layer])
        own_gate = lax.all_to_all(gates, "expert", split_axis=1, concat_axis=0, tiled=True)
        everyone = lax.all_gather(normed, "expert", axis=0, tiled=True)
        projected = jnp.dot(everyone, gate_ups[layer], preferred_element_type=jnp.float32)
        hidden = (
            jax.nn.silu(projected[:, :half_width]) * projected[:, half_width:]
        ).astype(jnp.bfloat16)
        answer = jnp.dot(hidden, downs[layer], preferred_element_type=jnp.float32)
        part = (answer * own_gate).astype(jnp.bfloat16)
        mixture = lax.psum_scatter(part, "expert", scatter_dimension=0, tiled=True)
        rows = (rows.astype(jnp.float32) + mixture.astype(jnp.float32)).astype(jnp.bfloat16)
    return rows[None], contrastive(rows, pair_index, topic_ids)


LANES = 128
MESH = pl.DeviceIdType.MESH


def sections_kernel(
    sizes, tokens, routing, guide, gate_up, down, final, passages,
    rows, guides, ups, downs, spread, parts, first_in, second_in, third_in, embeds,
    guide_sem, up_sem, down_sem, swap_sem, out_send, out_recv, back_send, back_recv,
    emb_send, emb_recv, pair_sem,
):
    layers, experts, depth, row_count, width = sizes
    half_rows = row_count // 2
    half_width = down.shape[2]
    core, me = lax.axis_index("segment"), lax.axis_index("expert")
    z, column = me // 4, me % 4
    y, x = column // 2, column % 2
    beside_x, beside_y = y * 2 + 1 - x, (1 - y) * 2 + x
    across = (1 - y) * 2 + 1 - x
    near, far = (beside_y, beside_x), (beside_x, beside_y)

    barrier = pltpu.get_barrier_semaphore()
    for step in range(1, experts):
        pl.semaphore_signal(
            barrier, inc=1, device_id=(core, (me + step) % experts), device_id_type=MESH
        )
    pl.semaphore_signal(barrier, inc=1, device_id=(1 - core, me), device_id_type=MESH)
    pl.semaphore_wait(barrier, experts)

    def remote(src, dst, sent, received, device):
        return pltpu.make_async_remote_copy(
            src_ref=src, dst_ref=dst, send_sem=sent, recv_sem=received,
            device_id=device, device_id_type=MESH,
        )

    weights = ((guide, guides, guide_sem), (gate_up.at[0, 0], ups, up_sem),
               (down.at[0, 0], downs, down_sem))
    swaps = []
    for i, (src, dst, sem) in enumerate(weights):
        pltpu.make_async_copy(src, dst.at[core], sem.at[core]).start()
        swap = remote(src, dst.at[core], swap_sem.at[i], sem.at[core], (1 - core, me))
        swap.start()
        swaps.append(swap)

    rows[...] = tokens[core]

    def landed(i, layer):
        src, dst, sem = weights[i]
        pltpu.make_async_copy(src, dst.at[layer], sem.at[layer]).wait()

    def layer_body(layer, carry):
        landed(0, layer)
        widened = rows[...].astype(jnp.float32)
        gain = guides[layer, pl.ds(LANES, 16), :][:1].astype(jnp.float32)
        normed = (
            widened
            * lax.rsqrt(jnp.mean(widened * widened, axis=1, keepdims=True) + EPSILON)
            * gain
        ).astype(jnp.bfloat16)
        logits = lax.dot_general(
            normed, guides[layer, pl.ds(0, LANES), :], (((1,), (1,)), ((), ())),
            preferred_element_type=jnp.float32,
        )
        lane = lax.broadcasted_iota(jnp.int32, (row_count, LANES), 1)
        routes = routing[layer, core]
        named = lane < 0
        for k in range(routes.shape[1]):
            named = named | (routes[:, k : k + 1] == lane % experts)
        raised = jnp.where(named, jnp.exp(logits), 0.0)
        gates = raised / jnp.sum(jnp.where(lane < experts, raised, 0.0), axis=1, keepdims=True)
        coarse = gates.astype(jnp.bfloat16).astype(jnp.float32)
        coded = jnp.where(
            lane < experts, coarse, jnp.where(lane < 2 * experts, gates - coarse, 0.0)
        ).astype(jnp.bfloat16)
        for h in range(2):
            here = slice(h * half_rows, (h + 1) * half_rows)
            spread[layer, h, column, z, :, pl.ds(0, width)] = normed[here]
            spread[layer, h, column, z, :, pl.ds(width, LANES)] = coded[here]

        sends = []

        def pass_on(h, block_column, block_z, device):
            slot = spread.at[layer, h, block_column, block_z]
            number = sum(1 for g, _ in sends if g == h)
            copy = remote(
                slot, slot, out_send.at[layer, h, number],
                out_recv.at[layer, h, block_column, block_z], (core, device),
            )
            copy.start()
            sends.append((h, copy))

        def arrived(h, block_column, block_z):
            slot = spread.at[layer, h, block_column, block_z]
            remote(
                slot, slot, out_send.at[layer, h, 0],
                out_recv.at[layer, h, block_column, block_z], (core, me),
            ).wait_recv()

        for h in range(2):
            pass_on(h, column, z, z * 4 + near[h])
        for step in range(1, depth):
            for h in range(2):
                pass_on(h, column, z, (z + step) % depth * 4 + column)
        for step in range(1, depth):
            for h in range(2):
                arrived(h, column, (z + depth - step) % depth)
                pass_on(h, column, (z + depth - step) % depth, z * 4 + near[h])
        for step in range(depth):
            for h in range(2):
                pass_on(h, column, (z + depth - step) % depth, z * 4 + far[h])
        landed(1, layer)
        landed(2, layer)

        def answer(columns):
            held = [spread[layer, h, columns[h]].reshape(depth * half_rows, -1) for h in range(2)]
            both = jnp.concatenate([b[:, :width] for b in held], axis=0)
            codes = jnp.concatenate([b[:, width:] for b in held], axis=0).astype(jnp.float32)
            mine = lax.broadcasted_iota(jnp.int32, codes.shape, 1) % experts == me
            gate = jnp.sum(jnp.where(mine, codes, 0.0), axis=1, keepdims=True)
            projected = jnp.dot(both, ups[layer], preferred_element_type=jnp.float32)
            lifted = projected[:, :half_width]
            hidden = (
                lifted / (1.0 + jnp.exp(-lifted)) * projected[:, half_width:]
            ).astype(jnp.bfloat16)
            result = jnp.dot(hidden, downs[layer], preferred_element_type=jnp.float32)
            part = (result * gate).astype(jnp.bfloat16)
            part = part.reshape(2, depth, half_rows, width)
            for h in range(2):
                parts[layer, h, columns[h]] = part[h]

        backs = []

        def send_back(h, src, dst, received, device):
            number = sum(1 for g, _ in backs if g == h)
            copy = remote(
                src, dst, back_send.at[layer, h, number], back_recv.at[layer, h, received],
                (core, device),
            )
            copy.start()
            backs.append((h, copy))

        def came_back(h, dst, received):
            remote(
                dst, dst, back_send.at[layer, h, 0], back_recv.at[layer, h, received], (core, me)
            ).wait_recv()

        answer((column, column))
        for step in range(depth):
            for h in range(2):
                block = (z + depth - step) % depth
                arrived(h, near[h], block)
                pass_on(h, near[h], block, z * 4 + far[h])
        answer(near)
        for step in range(depth):
            for h in range(2):
                block = (z + step) % depth
                send_back(
                    h, parts.at[layer, h, near[h], block], first_in.at[layer, h, 0, block],
                    block, z * 4 + near[h],
                )
        for step in range(depth):
            for h in range(2):
                arrived(h, far[h], (z + depth - step) % depth)
        answer(far)
        for step in range(depth):
            for h in range(2):
                arrived(h, across, (z + depth - step) % depth)
        answer((across, across))
        for step in range(1, depth + 1):
            for h in range(2):
                block = (z + step) % depth
                send_back(
                    h, parts.at[layer, h, across, block], first_in.at[layer, h, 1, block],
                    depth + block, z * 4 + near[h],
                )
        for step in range(1, depth + 1):
            for h in range(2):
                block = (z + step) % depth
                came_back(h, first_in.at[layer, h, 1, block], depth + block)
                parts[layer, h, far[h], block] = (
                    parts[layer, h, far[h], block].astype(jnp.float32)
                    + first_in[layer, h, 1, block].astype(jnp.float32)
                ).astype(jnp.bfloat16)
                send_back(
                    h, parts.at[layer, h, far[h], block], second_in.at[layer, h, block],
                    2 * depth + block, z * 4 + far[h],
                )
        for step in range(1, depth + 1):
            for h in range(2):
                block = (z + step) % depth
                came_back(h, first_in.at[layer, h, 0, block], block)
                came_back(h, second_in.at[layer, h, block], 2 * depth + block)
                total = (
                    parts[layer, h, column, block].astype(jnp.float32)
                    + first_in[layer, h, 0, block].astype(jnp.float32)
                    + second_in[layer, h, block].astype(jnp.float32)
                )
                if step < depth:
                    parts[layer, h, column, block] = total.astype(jnp.bfloat16)
                    send_back(
                        h, parts.at[layer, h, column, block], third_in.at[layer, h, z],
                        3 * depth + z, block * 4 + column,
                    )
                    continue
                for other in range(1, depth):
                    source = (z + depth - other) % depth
                    came_back(h, third_in.at[layer, h, source], 3 * depth + source)
                    total = total + third_in[layer, h, source].astype(jnp.float32)
                here = pl.ds(h * half_rows, half_rows)
                rows[here, :] = (rows[here, :].astype(jnp.float32) + total).astype(jnp.bfloat16)
        for _, copy in sends + backs:
            copy.wait_send()
        return carry

    lax.fori_loop(0, layers, layer_body, 0)

    final[...] = rows[...]
    pooled = jnp.mean(rows[...].astype(jnp.float32).reshape(-1, SEQ, width), axis=1)
    embedded = pooled * lax.rsqrt(jnp.sum(pooled * pooled, axis=1, keepdims=True) + EPSILON)
    embedded = embedded.astype(jnp.bfloat16).astype(jnp.float32)
    half_count, chunk = embedded.shape[0] // 2, embeds.shape[3]
    per_row = width // chunk
    for i in range(half_count * per_row):
        j = half_count + i // per_row
        first = i % per_row * chunk
        embeds[core, me, pl.ds(i, 1), :] = embedded[j : j + 1, first : first + chunk]
    slot = embeds.at[core, me]
    copies = []
    for step in range(1, experts):
        copy = remote(
            slot, slot, emb_send.at[step - 1], emb_recv.at[me], (core, (me + step) % experts)
        )
        copy.start()
        copies.append(copy)
    for step in range(1, experts):
        source = (me + step) % experts
        other = embeds.at[core, source]
        remote(other, other, emb_send.at[0], emb_recv.at[source], (core, me)).wait_recv()
    swap = remote(
        embeds.at[core], embeds.at[core], pair_sem.at[0], pair_sem.at[1], (1 - core, me)
    )
    swap.start()
    theirs = embeds.at[1 - core]
    remote(theirs, theirs, pair_sem.at[0], pair_sem.at[1], (1 - core, me)).wait_recv()
    swap.wait_send()
    for copy in copies + swaps:
        copy.wait_send()
    passages[...] = embeds[...]


def sections(
    tokens, routing, norm_gain, router_weight, expert_gate_up, expert_down, pair_index, topic_ids
):
    layers, experts = routing.shape[0], router_weight.shape[2]
    _, row_count, width = tokens.shape
    depth, half_rows, ff = experts // 4, row_count // 2, expert_down.shape[2]
    pooled_count = row_count // SEQ // 2
    chunk = pooled_count * width // 8
    guide = jnp.concatenate(
        [
            jnp.tile(router_weight[0].T, (LANES // experts, 1)),
            jnp.broadcast_to(norm_gain, (16, width)),
        ]
    )
    vmem, bf16 = pltpu.VMEM, jnp.bfloat16
    dma = pltpu.SemaphoreType.DMA
    block = (half_rows, width)
    in_vmem, anywhere = pl.BlockSpec(memory_space=vmem), pl.BlockSpec(memory_space=pl.ANY)
    final, passages = pl.pallas_call(
        functools.partial(sections_kernel, (layers, experts, depth, row_count, width)),
        out_shape=(
            jax.ShapeDtypeStruct((row_count, width), bf16),
            jax.ShapeDtypeStruct((2, experts, 8, chunk), jnp.float32),
        ),
        in_specs=[in_vmem, in_vmem, anywhere, anywhere, anywhere],
        out_specs=(in_vmem, in_vmem),
        scratch_shapes=[
            vmem((row_count, width), bf16),
            vmem((layers, LANES + 16, width), bf16),
            vmem((layers, width, 2 * ff), bf16),
            vmem((layers, ff, width), bf16),
            vmem((layers, 2, 4, depth, half_rows, width + LANES), bf16),
            vmem((layers, 2, 4, depth, *block), bf16),
            vmem((layers, 2, 2, depth, *block), bf16),
            vmem((layers, 2, depth, *block), bf16),
            vmem((layers, 2, depth, *block), bf16),
            vmem((2, experts, 8, chunk), jnp.float32),
            dma((layers,)),
            dma((layers,)),
            dma((layers,)),
            dma((3,)),
            dma((layers, 2, experts - 1)),
            dma((layers, 2, 4, depth)),
            dma((layers, 2, experts - 1)),
            dma((layers, 2, experts)),
            dma((experts - 1,)),
            dma((experts,)),
            dma((2,)),
        ],
        compiler_params=pltpu.CompilerParams(
            collective_id=0, has_side_effects=True, vmem_limit_bytes=56 * 1024 * 1024
        ),
    )(tokens, routing, guide, expert_gate_up, expert_down)
    return final[None], contrastive(final, pair_index, topic_ids, passages.reshape(-1, width).astype(bf16))


def solution(mesh):
    in_specs = (
        P(None, "expert", None),
        P(None, None, "expert", None),
        P("segment", None),
        P("segment", None, None),
        P("segment", "expert", None, None),
        P("segment", "expert", None, None),
        P(),
        P(),
    )
    out_specs = (P("segment", "expert", None), P(("segment", "expert")))
    experts = mesh.shape["expert"]
    fits = experts % 4 == 0 and experts * 2 <= 32 and mesh.shape["segment"] == 2
    return jax.shard_map(sections if fits else gathered, mesh=mesh, in_specs=in_specs, out_specs=out_specs, check_vma=False)
```

```python
import functools

import jax
import jax.numpy as jnp
from jax import lax
from jax.experimental import pallas as pl
from jax.experimental.pallas import tpu as pltpu
from jax.sharding import PartitionSpec as P

SEQ = 16


EPSILON = 1e-06
SOFTMAX_WARMTH = 0.05


def pooled_embeddings(final_rows):
    widened = final_rows.astype(jnp.float32)
    pooled = jnp.mean(widened.reshape(-1, SEQ, widened.shape[1]), axis=1)
    return (pooled * lax.rsqrt(jnp.sum(pooled * pooled, axis=1, keepdims=True) + EPSILON)).astype(
        jnp.bfloat16
    )


def normalised(rows, gain):
    widened = rows.astype(jnp.float32)
    return (
        widened
        * lax.rsqrt(jnp.mean(widened * widened, axis=1, keepdims=True) + EPSILON)
        * gain.astype(jnp.float32)
    ).astype(jnp.bfloat16)


def dense_gates(normed, routes, router_weight):
    expert_count = router_weight.shape[1]
    logits = jnp.dot(normed, router_weight, preferred_element_type=jnp.float32)
    experts = jnp.arange(expert_count, dtype=jnp.int32)
    named = jnp.any(routes[:, :, None] == experts[None, None, :], axis=1)
    raised = jnp.where(named, jnp.exp(logits), 0.0)
    return raised / jnp.sum(raised, axis=1, keepdims=True)


def contrastive(final_rows, pair_index, topic_ids, passages=None):
    embedded = pooled_embeddings(final_rows)
    half_count = embedded.shape[0] // 2
    own_queries = embedded[:half_count]
    if passages is None:
        passages = lax.all_gather(embedded[half_count:], ("segment", "expert"), axis=0, tiled=True)
    device_flat = lax.axis_index(("segment", "expert"))
    positive = lax.dynamic_slice_in_dim(pair_index, device_flat * half_count, half_count)
    columns = jnp.arange(topic_ids.shape[0], dtype=jnp.int32)
    is_positive = positive[:, None] == columns[None, :]
    positive_topic = jnp.sum(jnp.where(is_positive, topic_ids[None, :], 0), axis=1)
    kept = is_positive | (topic_ids[None, :] != positive_topic[:, None])
    scores = (
        jnp.dot(own_queries, passages.T, preferred_element_type=jnp.float32) / SOFTMAX_WARMTH
    )
    partition = jnp.sum(jnp.where(kept, jnp.exp(scores), 0.0), axis=1)
    return jnp.log(partition) - jnp.sum(jnp.where(is_positive, scores, 0.0), axis=1)


def gathered(
    tokens, routing, norm_gain, router_weight, expert_gate_up, expert_down, pair_index, topic_ids
):
    segment_index = lax.axis_index("segment")
    expert_index = lax.axis_index("expert")
    gains = lax.all_gather(norm_gain, "segment", axis=0, tiled=True)
    routers = lax.all_gather(router_weight, "segment", axis=0, tiled=True)

    def by_layer(own):
        other = lax.ppermute(own, "segment", [(0, 1), (1, 0)])
        first = segment_index == 0
        return jnp.where(first, own, other), jnp.where(first, other, own)

    gate_ups = by_layer(expert_gate_up[0, 0])
    downs = by_layer(expert_down[0, 0])
    rows = lax.dynamic_index_in_dim(tokens, segment_index, 0, keepdims=False)
    micro_routes = lax.dynamic_index_in_dim(routing, segment_index, 1, keepdims=False)
    half_width = expert_down.shape[2]
    for layer in range(routing.shape[0]):
        normed = normalised(rows, gains[layer])
        gates = dense_gates(normed, micro_routes[layer], routers[layer])
        own_gate = lax.all_to_all(gates, "expert", split_axis=1, concat_axis=0, tiled=True)
        everyone = lax.all_gather(normed, "expert", axis=0, tiled=True)
        projected = jnp.dot(everyone, gate_ups[layer], preferred_element_type=jnp.float32)
        hidden = (
            jax.nn.silu(projected[:, :half_width]) * projected[:, half_width:]
        ).astype(jnp.bfloat16)
        answer = jnp.dot(hidden, downs[layer], preferred_element_type=jnp.float32)
        part = (answer * own_gate).astype(jnp.bfloat16)
        mixture = lax.psum_scatter(part, "expert", scatter_dimension=0, tiled=True)
        rows = (rows.astype(jnp.float32) + mixture.astype(jnp.float32)).astype(jnp.bfloat16)
    return rows[None], contrastive(rows, pair_index, topic_ids)


LANES = 128
MESH = pl.DeviceIdType.MESH


def sections_kernel(
    sizes, tokens, routing, guide, gate_up, down, final, passages,
    rows, guides, ups, downs, spread, parts, first_in, second_in, third_in, embeds,
    guide_sem, up_sem, down_sem, swap_sem, out_send, out_recv, back_send, back_recv,
    emb_send, emb_recv, pair_sem,
):
    layers, experts, depth, row_count, width = sizes
    half_rows = row_count // 2
    half_width = down.shape[2]
    core, me = lax.axis_index("segment"), lax.axis_index("expert")
    z, column = me // 4, me % 4
    y, x = column // 2, column % 2
    beside_x, beside_y = y * 2 + 1 - x, (1 - y) * 2 + x
    across = (1 - y) * 2 + 1 - x
    order = [z, z + 1 - 2 * (z % 2), (z + 2) % 4, 3 - z][:depth]
    near, far = (beside_y, beside_x), (beside_x, beside_y)

    barrier = pltpu.get_barrier_semaphore()
    for step in range(1, experts):
        pl.semaphore_signal(
            barrier, inc=1, device_id=(core, (me + step) % experts), device_id_type=MESH
        )
    pl.semaphore_signal(barrier, inc=1, device_id=(1 - core, me), device_id_type=MESH)
    pl.semaphore_wait(barrier, experts)

    def remote(src, dst, sent, received, device):
        return pltpu.make_async_remote_copy(
            src_ref=src, dst_ref=dst, send_sem=sent, recv_sem=received,
            device_id=device, device_id_type=MESH,
        )

    weights = ((guide, guides, guide_sem), (gate_up.at[0, 0], ups, up_sem),
               (down.at[0, 0], downs, down_sem))
    swaps = []

    def share(i):
        src, dst, sem = weights[i]
        pltpu.make_async_copy(src, dst.at[core], sem.at[core]).start()
        swap = remote(src, dst.at[core], swap_sem.at[i], sem.at[core], (1 - core, me))
        swap.start()
        swaps.append(swap)

    def landed(i, layer):
        src, dst, sem = weights[i]
        pltpu.make_async_copy(src, dst.at[layer], sem.at[layer]).wait()

    share(0)
    rows[...] = tokens[core]
    for layer in range(layers):
        landed(0, layer)
    share(1)
    share(2)

    def layer_body(layer, carry):
        widened = rows[...].astype(jnp.float32)
        gain = guides[layer, pl.ds(LANES, 16), :][:1].astype(jnp.float32)
        normed = (
            widened
            * lax.rsqrt(jnp.mean(widened * widened, axis=1, keepdims=True) + EPSILON)
            * gain
        ).astype(jnp.bfloat16)
        logits = lax.dot_general(
            normed, guides[layer, pl.ds(0, LANES), :], (((1,), (1,)), ((), ())),
            preferred_element_type=jnp.float32,
        )
        lane = lax.broadcasted_iota(jnp.int32, (row_count, LANES), 1)
        routes = routing[layer, core]
        named = lane < 0
        for k in range(routes.shape[1]):
            named = named | (routes[:, k : k + 1] == lane % experts)
        raised = jnp.where(named, jnp.exp(logits), 0.0)
        gates = raised / jnp.sum(jnp.where(lane < experts, raised, 0.0), axis=1, keepdims=True)
        coarse = gates.astype(jnp.bfloat16).astype(jnp.float32)
        coded = jnp.where(
            lane < experts, coarse, jnp.where(lane < 2 * experts, gates - coarse, 0.0)
        ).astype(jnp.bfloat16)
        for h in range(2):
            here = slice(h * half_rows, (h + 1) * half_rows)
            spread[layer, h, column, z, :, pl.ds(0, width)] = normed[here]
            spread[layer, h, column, z, :, pl.ds(width, LANES)] = coded[here]

        sends = []

        def pass_on(h, block_column, block_z, device):
            slot = spread.at[layer, h, block_column, block_z]
            number = sum(1 for g, _ in sends if g == h)
            copy = remote(
                slot, slot, out_send.at[layer, h, number],
                out_recv.at[layer, h, block_column, block_z], (core, device),
            )
            copy.start()
            sends.append((h, copy))

        def arrived(h, block_column, block_z):
            slot = spread.at[layer, h, block_column, block_z]
            remote(
                slot, slot, out_send.at[layer, h, 0],
                out_recv.at[layer, h, block_column, block_z], (core, me),
            ).wait_recv()

        for block in order[1:]:
            for h in range(2):
                pass_on(h, column, z, block * 4 + column)
        for h in range(2):
            pass_on(h, column, z, z * 4 + near[h])
            pass_on(h, column, z, z * 4 + far[h])
        for step in range(1, depth + 1):
            for h in range(2):
                if step < depth:
                    arrived(h, column, order[step])
                    pass_on(h, column, order[step], z * 4 + near[h])
                    pass_on(h, column, order[step], z * 4 + far[h])
            for h in range(2):
                arrived(h, near[h], order[step - 1])
                pass_on(h, near[h], order[step - 1], z * 4 + far[h])
        landed(1, layer)
        landed(2, layer)

        def answer(columns):
            held = [spread[layer, h, columns[h]].reshape(depth * half_rows, -1) for h in range(2)]
            both = jnp.concatenate([b[:, :width] for b in held], axis=0)
            codes = jnp.concatenate([b[:, width:] for b in held], axis=0).astype(jnp.float32)
            mine = lax.broadcasted_iota(jnp.int32, codes.shape, 1) % experts == me
            gate = jnp.sum(jnp.where(mine, codes, 0.0), axis=1, keepdims=True)
            projected = jnp.dot(both, ups[layer], preferred_element_type=jnp.float32)
            lifted = projected[:, :half_width]
            hidden = (
                lifted / (1.0 + jnp.exp(-lifted)) * projected[:, half_width:]
            ).astype(jnp.bfloat16)
            result = jnp.dot(hidden, downs[layer], preferred_element_type=jnp.float32)
            part = (result * gate).astype(jnp.bfloat16)
            part = part.reshape(2, depth, half_rows, width)
            for h in range(2):
                parts[layer, h, columns[h]] = part[h]

        backs = []

        def send_back(h, src, dst, received, device):
            number = sum(1 for g, _ in backs if g == h)
            copy = remote(
                src, dst, back_send.at[layer, h, number], back_recv.at[layer, h, received],
                (core, device),
            )
            copy.start()
            backs.append((h, copy))

        def came_back(h, dst, received):
            remote(
                dst, dst, back_send.at[layer, h, 0], back_recv.at[layer, h, received], (core, me)
            ).wait_recv()

        answer((column, column))
        answer(near)
        for step in range(depth):
            for h in range(2):
                block = order[step % depth]
                send_back(
                    h, parts.at[layer, h, near[h], block], first_in.at[layer, h, 0, block],
                    block, z * 4 + near[h],
                )
        for step in range(depth):
            for h in range(2):
                arrived(h, far[h], order[step])
        answer(far)
        for step in range(depth):
            for h in range(2):
                arrived(h, across, order[step])
        answer((across, across))
        for step in range(1, depth + 1):
            for h in range(2):
                block = order[step % depth]
                send_back(
                    h, parts.at[layer, h, across, block], first_in.at[layer, h, 1, block],
                    depth + block, z * 4 + near[h],
                )
        for step in range(1, depth + 1):
            for h in range(2):
                block = order[step % depth]
                came_back(h, first_in.at[layer, h, 1, block], depth + block)
                parts[layer, h, far[h], block] = (
                    parts[layer, h, far[h], block].astype(jnp.float32)
                    + first_in[layer, h, 1, block].astype(jnp.float32)
                ).astype(jnp.bfloat16)
                send_back(
                    h, parts.at[layer, h, far[h], block], second_in.at[layer, h, block],
                    2 * depth + block, z * 4 + far[h],
                )
        for step in range(1, depth + 1):
            for h in range(2):
                block = order[step % depth]
                came_back(h, first_in.at[layer, h, 0, block], block)
                came_back(h, second_in.at[layer, h, block], 2 * depth + block)
                total = (
                    parts[layer, h, column, block].astype(jnp.float32)
                    + first_in[layer, h, 0, block].astype(jnp.float32)
                    + second_in[layer, h, block].astype(jnp.float32)
                )
                if step < depth:
                    parts[layer, h, column, block] = total.astype(jnp.bfloat16)
                    send_back(
                        h, parts.at[layer, h, column, block], third_in.at[layer, h, z],
                        3 * depth + z, block * 4 + column,
                    )
                    continue
                for other in range(1, depth):
                    source = order[other]
                    came_back(h, third_in.at[layer, h, source], 3 * depth + source)
                    total = total + third_in[layer, h, source].astype(jnp.float32)
                here = pl.ds(h * half_rows, half_rows)
                rows[here, :] = (rows[here, :].astype(jnp.float32) + total).astype(jnp.bfloat16)
        for _, copy in sends + backs:
            copy.wait_send()
        return carry

    lax.fori_loop(0, layers, layer_body, 0)

    final[...] = rows[...]
    pooled = jnp.mean(rows[...].astype(jnp.float32).reshape(-1, SEQ, width), axis=1)
    embedded = pooled * lax.rsqrt(jnp.sum(pooled * pooled, axis=1, keepdims=True) + EPSILON)
    embedded = embedded.astype(jnp.bfloat16).astype(jnp.float32)
    half_count, chunk = embedded.shape[0] // 2, embeds.shape[3]
    per_row = width // chunk
    for i in range(half_count * per_row):
        j = half_count + i // per_row
        first = i % per_row * chunk
        embeds[core, me, pl.ds(i, 1), :] = embedded[j : j + 1, first : first + chunk]
    slot = embeds.at[core, me]
    copies = []
    for step in range(1, experts):
        copy = remote(
            slot, slot, emb_send.at[step - 1], emb_recv.at[me], (core, (me + step) % experts)
        )
        copy.start()
        copies.append(copy)
    for step in range(1, experts):
        source = (me + step) % experts
        other = embeds.at[core, source]
        remote(other, other, emb_send.at[0], emb_recv.at[source], (core, me)).wait_recv()
    swap = remote(
        embeds.at[core], embeds.at[core], pair_sem.at[0], pair_sem.at[1], (1 - core, me)
    )
    swap.start()
    theirs = embeds.at[1 - core]
    remote(theirs, theirs, pair_sem.at[0], pair_sem.at[1], (1 - core, me)).wait_recv()
    swap.wait_send()
    for copy in copies + swaps:
        copy.wait_send()
    passages[...] = embeds[...]


def sections(
    tokens, routing, norm_gain, router_weight, expert_gate_up, expert_down, pair_index, topic_ids
):
    layers, experts = routing.shape[0], router_weight.shape[2]
    _, row_count, width = tokens.shape
    depth, half_rows, ff = experts // 4, row_count // 2, expert_down.shape[2]
    pooled_count = row_count // SEQ // 2
    chunk = pooled_count * width // 8
    guide = jnp.concatenate(
        [
            jnp.tile(router_weight[0].T, (LANES // experts, 1)),
            jnp.broadcast_to(norm_gain, (16, width)),
        ]
    )
    vmem, bf16 = pltpu.VMEM, jnp.bfloat16
    dma = pltpu.SemaphoreType.DMA
    block = (half_rows, width)
    in_vmem, anywhere = pl.BlockSpec(memory_space=vmem), pl.BlockSpec(memory_space=pl.ANY)
    final, passages = pl.pallas_call(
        functools.partial(sections_kernel, (layers, experts, depth, row_count, width)),
        out_shape=(
            jax.ShapeDtypeStruct((row_count, width), bf16),
            jax.ShapeDtypeStruct((2, experts, 8, chunk), jnp.float32),
        ),
        in_specs=[in_vmem, in_vmem, anywhere, anywhere, anywhere],
        out_specs=(in_vmem, in_vmem),
        scratch_shapes=[
            vmem((row_count, width), bf16),
            vmem((layers, LANES + 16, width), bf16),
            vmem((layers, width, 2 * ff), bf16),
            vmem((layers, ff, width), bf16),
            vmem((layers, 2, 4, depth, half_rows, width + LANES), bf16),
            vmem((layers, 2, 4, depth, *block), bf16),
            vmem((layers, 2, 2, depth, *block), bf16),
            vmem((layers, 2, depth, *block), bf16),
            vmem((layers, 2, depth, *block), bf16),
            vmem((2, experts, 8, chunk), jnp.float32),
            dma((layers,)),
            dma((layers,)),
            dma((layers,)),
            dma((3,)),
            dma((layers, 2, experts - 1)),
            dma((layers, 2, 4, depth)),
            dma((layers, 2, experts - 1)),
            dma((layers, 2, experts)),
            dma((experts - 1,)),
            dma((experts,)),
            dma((2,)),
        ],
        compiler_params=pltpu.CompilerParams(
            collective_id=0, has_side_effects=True, vmem_limit_bytes=56 * 1024 * 1024
        ),
    )(tokens, routing, guide, expert_gate_up, expert_down)
    return final[None], contrastive(final, pair_index, topic_ids, passages.reshape(-1, width).astype(bf16))


def solution(mesh):
    in_specs = (
        P(None, "expert", None),
        P(None, None, "expert", None),
        P("segment", None),
        P("segment", None, None),
        P("segment", "expert", None, None),
        P("segment", "expert", None, None),
        P(),
        P(),
    )
    out_specs = (P("segment", "expert", None), P(("segment", "expert")))
    experts = mesh.shape["expert"]
    fits = experts in (4, 8, 16) and mesh.shape["segment"] == 2
    return jax.shard_map(sections if fits else gathered, mesh=mesh, in_specs=in_specs, out_specs=out_specs, check_vma=False)
```

```python
import functools

import jax
import jax.numpy as jnp
from jax import lax
from jax.experimental import pallas as pl
from jax.experimental.pallas import tpu as pltpu
from jax.sharding import PartitionSpec as P

SEQ = 16


EPSILON = 1e-06
SOFTMAX_WARMTH = 0.05


def pooled_embeddings(final_rows):
    widened = final_rows.astype(jnp.float32)
    pooled = jnp.mean(widened.reshape(-1, SEQ, widened.shape[1]), axis=1)
    return (pooled * lax.rsqrt(jnp.sum(pooled * pooled, axis=1, keepdims=True) + EPSILON)).astype(
        jnp.bfloat16
    )


def normalised(rows, gain):
    widened = rows.astype(jnp.float32)
    return (
        widened
        * lax.rsqrt(jnp.mean(widened * widened, axis=1, keepdims=True) + EPSILON)
        * gain.astype(jnp.float32)
    ).astype(jnp.bfloat16)


def dense_gates(normed, routes, router_weight):
    expert_count = router_weight.shape[1]
    logits = jnp.dot(normed, router_weight, preferred_element_type=jnp.float32)
    experts = jnp.arange(expert_count, dtype=jnp.int32)
    named = jnp.any(routes[:, :, None] == experts[None, None, :], axis=1)
    raised = jnp.where(named, jnp.exp(logits), 0.0)
    return raised / jnp.sum(raised, axis=1, keepdims=True)


def contrastive(final_rows, pair_index, topic_ids, passages=None):
    embedded = pooled_embeddings(final_rows)
    half_count = embedded.shape[0] // 2
    own_queries = embedded[:half_count]
    if passages is None:
        passages = lax.all_gather(embedded[half_count:], ("segment", "expert"), axis=0, tiled=True)
    device_flat = lax.axis_index(("segment", "expert"))
    positive = lax.dynamic_slice_in_dim(pair_index, device_flat * half_count, half_count)
    columns = jnp.arange(topic_ids.shape[0], dtype=jnp.int32)
    is_positive = positive[:, None] == columns[None, :]
    positive_topic = jnp.sum(jnp.where(is_positive, topic_ids[None, :], 0), axis=1)
    kept = is_positive | (topic_ids[None, :] != positive_topic[:, None])
    scores = (
        jnp.dot(own_queries, passages.T, preferred_element_type=jnp.float32) / SOFTMAX_WARMTH
    )
    partition = jnp.sum(jnp.where(kept, jnp.exp(scores), 0.0), axis=1)
    return jnp.log(partition) - jnp.sum(jnp.where(is_positive, scores, 0.0), axis=1)


def gathered(
    tokens, routing, norm_gain, router_weight, expert_gate_up, expert_down, pair_index, topic_ids
):
    segment_index = lax.axis_index("segment")
    expert_index = lax.axis_index("expert")
    gains = lax.all_gather(norm_gain, "segment", axis=0, tiled=True)
    routers = lax.all_gather(router_weight, "segment", axis=0, tiled=True)

    def by_layer(own):
        other = lax.ppermute(own, "segment", [(0, 1), (1, 0)])
        first = segment_index == 0
        return jnp.where(first, own, other), jnp.where(first, other, own)

    gate_ups = by_layer(expert_gate_up[0, 0])
    downs = by_layer(expert_down[0, 0])
    rows = lax.dynamic_index_in_dim(tokens, segment_index, 0, keepdims=False)
    micro_routes = lax.dynamic_index_in_dim(routing, segment_index, 1, keepdims=False)
    half_width = expert_down.shape[2]
    for layer in range(routing.shape[0]):
        normed = normalised(rows, gains[layer])
        gates = dense_gates(normed, micro_routes[layer], routers[layer])
        own_gate = lax.all_to_all(gates, "expert", split_axis=1, concat_axis=0, tiled=True)
        everyone = lax.all_gather(normed, "expert", axis=0, tiled=True)
        projected = jnp.dot(everyone, gate_ups[layer], preferred_element_type=jnp.float32)
        hidden = (
            jax.nn.silu(projected[:, :half_width]) * projected[:, half_width:]
        ).astype(jnp.bfloat16)
        answer = jnp.dot(hidden, downs[layer], preferred_element_type=jnp.float32)
        part = (answer * own_gate).astype(jnp.bfloat16)
        mixture = lax.psum_scatter(part, "expert", scatter_dimension=0, tiled=True)
        rows = (rows.astype(jnp.float32) + mixture.astype(jnp.float32)).astype(jnp.bfloat16)
    return rows[None], contrastive(rows, pair_index, topic_ids)


LANES = 128
MESH = pl.DeviceIdType.MESH


def sections_kernel(
    sizes, tokens, routing, guide, gate_up, down, final, passages,
    rows, guides, ups, downs, spread, parts, first_in, second_in, third_in, embeds,
    guide_sem, up_sem, down_sem, swap_sem, out_send, out_recv, back_send, back_recv,
    emb_send, emb_recv, pair_sem,
):
    layers, experts, depth, row_count, width = sizes
    half_rows = row_count // 2
    half_width = down.shape[2]
    core, me = lax.axis_index("segment"), lax.axis_index("expert")
    z, column = me // 4, me % 4
    y, x = column // 2, column % 2
    beside_x, beside_y = y * 2 + 1 - x, (1 - y) * 2 + x
    across = (1 - y) * 2 + 1 - x
    order = [z, z + 1 - 2 * (z % 2), (z + 2) % 4, 3 - z][:depth]
    near, far = (beside_y, beside_x), (beside_x, beside_y)

    barrier = pltpu.get_barrier_semaphore()
    for step in range(1, experts):
        pl.semaphore_signal(
            barrier, inc=1, device_id=(core, (me + step) % experts), device_id_type=MESH
        )
    pl.semaphore_signal(barrier, inc=1, device_id=(1 - core, me), device_id_type=MESH)
    pl.semaphore_wait(barrier, experts)

    def remote(src, dst, sent, received, device):
        return pltpu.make_async_remote_copy(
            src_ref=src, dst_ref=dst, send_sem=sent, recv_sem=received,
            device_id=device, device_id_type=MESH,
        )

    weights = ((guide, guides, guide_sem), (gate_up.at[0, 0], ups, up_sem),
               (down.at[0, 0], downs, down_sem))
    swaps = []

    def share(i):
        src, dst, sem = weights[i]
        pltpu.make_async_copy(src, dst.at[core], sem.at[core]).start()
        swap = remote(src, dst.at[core], swap_sem.at[i], sem.at[core], (1 - core, me))
        swap.start()
        swaps.append(swap)

    def landed(i, layer):
        src, dst, sem = weights[i]
        pltpu.make_async_copy(src, dst.at[layer], sem.at[layer]).wait()

    share(0)
    rows[...] = tokens[core]
    for layer in range(layers):
        landed(0, layer)
    share(1)
    share(2)

    def layer_body(layer, carry):
        widened = rows[...].astype(jnp.float32)
        gain = guides[layer, pl.ds(LANES, 16), :][:1].astype(jnp.float32)
        normed = (
            widened
            * lax.rsqrt(jnp.mean(widened * widened, axis=1, keepdims=True) + EPSILON)
            * gain
        ).astype(jnp.bfloat16)
        logits = lax.dot_general(
            normed, guides[layer, pl.ds(0, LANES), :], (((1,), (1,)), ((), ())),
            preferred_element_type=jnp.float32,
        )
        lane = lax.broadcasted_iota(jnp.int32, (row_count, LANES), 1)
        routes = routing[layer, core]
        named = lane < 0
        for k in range(routes.shape[1]):
            named = named | (routes[:, k : k + 1] == lane % experts)
        raised = jnp.where(named, jnp.exp(logits), 0.0)
        gates = raised / jnp.sum(jnp.where(lane < experts, raised, 0.0), axis=1, keepdims=True)
        coarse = gates.astype(jnp.bfloat16).astype(jnp.float32)
        coded = jnp.where(
            lane < experts, coarse, jnp.where(lane < 2 * experts, gates - coarse, 0.0)
        ).astype(jnp.bfloat16)
        for h in range(2):
            here = slice(h * half_rows, (h + 1) * half_rows)
            spread[layer, h, column, z, :, pl.ds(0, width)] = normed[here]
            spread[layer, h, column, z, :, pl.ds(width, LANES)] = coded[here]

        sends = []

        def pass_on(h, block_column, block_z, device):
            slot = spread.at[layer, h, block_column, block_z]
            number = sum(1 for g, _ in sends if g == h)
            copy = remote(
                slot, slot, out_send.at[layer, h, number],
                out_recv.at[layer, h, block_column, block_z], (core, device),
            )
            copy.start()
            sends.append((h, copy))

        def arrived(h, block_column, block_z):
            slot = spread.at[layer, h, block_column, block_z]
            remote(
                slot, slot, out_send.at[layer, h, 0],
                out_recv.at[layer, h, block_column, block_z], (core, me),
            ).wait_recv()

        for block in order[1:]:
            for h in range(2):
                pass_on(h, column, z, block * 4 + column)
        for h in range(2):
            pass_on(h, column, z, z * 4 + near[h])
            pass_on(h, column, z, z * 4 + far[h])
        for step in range(1, depth + 1):
            for h in range(2):
                if step < depth:
                    arrived(h, column, order[step])
                    pass_on(h, column, order[step], z * 4 + near[h])
                    pass_on(h, column, order[step], z * 4 + far[h])
            for h in range(2):
                arrived(h, near[h], order[step - 1])
                pass_on(h, near[h], order[step - 1], z * 4 + far[h])
        landed(1, layer)
        landed(2, layer)

        def answer(columns):
            held = [spread[layer, h, columns[h]].reshape(depth * half_rows, -1) for h in range(2)]
            both = jnp.concatenate([b[:, :width] for b in held], axis=0)
            codes = jnp.concatenate([b[:, width:] for b in held], axis=0).astype(jnp.float32)
            mine = lax.broadcasted_iota(jnp.int32, codes.shape, 1) % experts == me
            gate = jnp.sum(jnp.where(mine, codes, 0.0), axis=1, keepdims=True)
            projected = jnp.dot(both, ups[layer], preferred_element_type=jnp.float32)
            lifted = projected[:, :half_width]
            hidden = (
                lifted / (1.0 + jnp.exp(-lifted)) * projected[:, half_width:]
            ).astype(jnp.bfloat16)
            result = jnp.dot(hidden, downs[layer], preferred_element_type=jnp.float32)
            part = (result * gate).astype(jnp.bfloat16)
            part = part.reshape(2, depth, half_rows, width)
            for h in range(2):
                parts[layer, h, columns[h]] = part[h]

        backs = []

        def send_back(h, src, dst, received, device):
            number = sum(1 for g, _ in backs if g == h)
            copy = remote(
                src, dst, back_send.at[layer, h, number], back_recv.at[layer, h, received],
                (core, device),
            )
            copy.start()
            backs.append((h, copy))

        def came_back(h, dst, received):
            remote(
                dst, dst, back_send.at[layer, h, 0], back_recv.at[layer, h, received], (core, me)
            ).wait_recv()

        answer((column, column))
        answer(near)
        for block in order[::-1]:
            for h in range(2):
                send_back(
                    h, parts.at[layer, h, near[h], block], first_in.at[layer, h, 0, block],
                    block, z * 4 + near[h],
                )
        for step in range(depth):
            for h in range(2):
                arrived(h, far[h], order[step])
        answer(far)
        for step in range(depth):
            for h in range(2):
                arrived(h, across, order[step])
        answer((across, across))
        for block in order[::-1]:
            for h in range(2):
                send_back(
                    h, parts.at[layer, h, across, block], first_in.at[layer, h, 1, block],
                    depth + block, z * 4 + near[h],
                )
        for step in range(depth + 1):
            for h in range(2):
                if step == depth:
                    continue
                block = order[depth - 1 - step]
                came_back(h, first_in.at[layer, h, 1, block], depth + block)
                parts[layer, h, far[h], block] = (
                    parts[layer, h, far[h], block].astype(jnp.float32)
                    + first_in[layer, h, 1, block].astype(jnp.float32)
                ).astype(jnp.bfloat16)
                send_back(
                    h, parts.at[layer, h, far[h], block], second_in.at[layer, h, block],
                    2 * depth + block, z * 4 + far[h],
                )
            for h in range(2):
                if step == 0:
                    continue
                block = order[depth - step]
                came_back(h, first_in.at[layer, h, 0, block], block)
                came_back(h, second_in.at[layer, h, block], 2 * depth + block)
                total = (
                    parts[layer, h, column, block].astype(jnp.float32)
                    + first_in[layer, h, 0, block].astype(jnp.float32)
                    + second_in[layer, h, block].astype(jnp.float32)
                )
                if step < depth:
                    parts[layer, h, column, block] = total.astype(jnp.bfloat16)
                    send_back(
                        h, parts.at[layer, h, column, block], third_in.at[layer, h, z],
                        3 * depth + z, block * 4 + column,
                    )
                    continue
                for other in range(1, depth):
                    source = order[other]
                    came_back(h, third_in.at[layer, h, source], 3 * depth + source)
                    total = total + third_in[layer, h, source].astype(jnp.float32)
                here = pl.ds(h * half_rows, half_rows)
                rows[here, :] = (rows[here, :].astype(jnp.float32) + total).astype(jnp.bfloat16)
        for _, copy in sends + backs:
            copy.wait_send()
        return carry

    lax.fori_loop(0, layers, layer_body, 0)

    final[...] = rows[...]
    pooled = jnp.mean(rows[...].astype(jnp.float32).reshape(-1, SEQ, width), axis=1)
    embedded = pooled * lax.rsqrt(jnp.sum(pooled * pooled, axis=1, keepdims=True) + EPSILON)
    embedded = embedded.astype(jnp.bfloat16).astype(jnp.float32)
    half_count, chunk = embedded.shape[0] // 2, embeds.shape[3]
    per_row = width // chunk
    for i in range(half_count * per_row):
        j = half_count + i // per_row
        first = i % per_row * chunk
        embeds[core, me, pl.ds(i, 1), :] = embedded[j : j + 1, first : first + chunk]
    slot = embeds.at[core, me]
    copies = []
    for step in range(1, experts):
        copy = remote(
            slot, slot, emb_send.at[step - 1], emb_recv.at[me], (core, (me + step) % experts)
        )
        copy.start()
        copies.append(copy)
    for step in range(1, experts):
        source = (me + step) % experts
        other = embeds.at[core, source]
        remote(other, other, emb_send.at[0], emb_recv.at[source], (core, me)).wait_recv()
    swap = remote(
        embeds.at[core], embeds.at[core], pair_sem.at[0], pair_sem.at[1], (1 - core, me)
    )
    swap.start()
    theirs = embeds.at[1 - core]
    remote(theirs, theirs, pair_sem.at[0], pair_sem.at[1], (1 - core, me)).wait_recv()
    swap.wait_send()
    for copy in copies + swaps:
        copy.wait_send()
    passages[...] = embeds[...]


def sections(
    tokens, routing, norm_gain, router_weight, expert_gate_up, expert_down, pair_index, topic_ids
):
    layers, experts = routing.shape[0], router_weight.shape[2]
    _, row_count, width = tokens.shape
    depth, half_rows, ff = experts // 4, row_count // 2, expert_down.shape[2]
    pooled_count = row_count // SEQ // 2
    chunk = pooled_count * width // 8
    guide = jnp.concatenate(
        [
            jnp.tile(router_weight[0].T, (LANES // experts, 1)),
            jnp.broadcast_to(norm_gain, (16, width)),
        ]
    )
    vmem, bf16 = pltpu.VMEM, jnp.bfloat16
    dma = pltpu.SemaphoreType.DMA
    block = (half_rows, width)
    in_vmem, anywhere = pl.BlockSpec(memory_space=vmem), pl.BlockSpec(memory_space=pl.ANY)
    final, passages = pl.pallas_call(
        functools.partial(sections_kernel, (layers, experts, depth, row_count, width)),
        out_shape=(
            jax.ShapeDtypeStruct((row_count, width), bf16),
            jax.ShapeDtypeStruct((2, experts, 8, chunk), jnp.float32),
        ),
        in_specs=[in_vmem, in_vmem, anywhere, anywhere, anywhere],
        out_specs=(in_vmem, in_vmem),
        scratch_shapes=[
            vmem((row_count, width), bf16),
            vmem((layers, LANES + 16, width), bf16),
            vmem((layers, width, 2 * ff), bf16),
            vmem((layers, ff, width), bf16),
            vmem((layers, 2, 4, depth, half_rows, width + LANES), bf16),
            vmem((layers, 2, 4, depth, *block), bf16),
            vmem((layers, 2, 2, depth, *block), bf16),
            vmem((layers, 2, depth, *block), bf16),
            vmem((layers, 2, depth, *block), bf16),
            vmem((2, experts, 8, chunk), jnp.float32),
            dma((layers,)),
            dma((layers,)),
            dma((layers,)),
            dma((3,)),
            dma((layers, 2, experts - 1)),
            dma((layers, 2, 4, depth)),
            dma((layers, 2, experts - 1)),
            dma((layers, 2, experts)),
            dma((experts - 1,)),
            dma((experts,)),
            dma((2,)),
        ],
        compiler_params=pltpu.CompilerParams(
            collective_id=0, has_side_effects=True, vmem_limit_bytes=56 * 1024 * 1024
        ),
    )(tokens, routing, guide, expert_gate_up, expert_down)
    return final[None], contrastive(final, pair_index, topic_ids, passages.reshape(-1, width).astype(bf16))


def solution(mesh):
    in_specs = (
        P(None, "expert", None),
        P(None, None, "expert", None),
        P("segment", None),
        P("segment", None, None),
        P("segment", "expert", None, None),
        P("segment", "expert", None, None),
        P(),
        P(),
    )
    out_specs = (P("segment", "expert", None), P(("segment", "expert")))
    experts = mesh.shape["expert"]
    fits = experts in (4, 8, 16) and mesh.shape["segment"] == 2
    return jax.shard_map(sections if fits else gathered, mesh=mesh, in_specs=in_specs, out_specs=out_specs, check_vma=False)
```
